32 devices in a mesh: groups: 2 (over y), neuron: 8 (over z, x), expert: 2 (over core).
Axes of the slice: x: 2, y: 2, z: 4, core: 2. Of those that a mesh axis runs over, the one named last changes fastest.
Arguments:
- tokens: bfloat16 [128, 4096], P(('groups', 'neuron', 'expert')), parts along dimension 0, may hold values from -6 to 6
- routes: int32 [128, 2], P(('groups', 'neuron', 'expert')), parts along dimension 0, may hold values from 0 to 7, as said below
- route_weights: int32 [128, 2], P(('groups', 'neuron', 'expert')), parts along dimension 0, may hold values from 6554 to 65535
- block_masks: int32 [128, 2, 4], P(('groups', 'neuron', 'expert')), parts along dimension 0, may hold values from 0 to 1073741823, as said below
- block_list: int32 [4, 120], P(('groups', 'expert')), parts along dimension 0, may hold values from 0 to 111, as said below
- gate_rows: bfloat16 [4, 15360, 4096], P(('groups', 'expert'), 'neuron'), parts along dimension 0, as said below
- up_rows: bfloat16 [4, 15360, 4096], P(('groups', 'expert'), 'neuron'), parts along dimension 0, as said below
- down_rows: bfloat16 [4, 15360, 4096], P(('groups', 'expert'), 'neuron'), parts along dimension 0, as said below
Outputs:
- moe_output: bfloat16 [128, 4096], P(('groups', 'neuron', 'expert')), parts along dimension 0
The draws below stay inside these ranges and needn't reach their ends.
There are 2 independent parts, one for each index of `groups`. The reference program is written for one: setup_inputs(seed, part) draws one part's arguments, and reference() takes and returns one part's arrays. A program takes and returns all parts, laid end to end along the dimension named above; each array names one. Nothing has to cross between parts.
Inputs may be any that keep to these rules, and one draw needn't show every extreme that they name: `routes`: each row names 2 different experts; in each aligned block of 8 rows every expert is named by exactly 2 rows. Bit i of word w of block_masks[t, r] marks row block 30 w + i of expert routes[t, r] as active; bits from 112 on are zero. A block that block_list places in two slots is active in every row that routes to its expert; any other block is active in exactly 1 of the 2 rows of an aligned block of 8 rows that route to its expert. `block_list`: slots are numbered along the neuron axis, 15 to a shard; every block of an expert sits in one slot, and 8 of them in two. `gate_rows`: the rows of slot s of expert e hold the block named by block_list[e, s]; two slots of one block hold equal rows. `up_rows`: as gate_rows. `down_rows`: as gate_rows.
All inputs are finite; a program needn't handle non-finite values.
Results may differ from the reference program's by a relative error of at most 0.005.
Values may be sent and summed in bfloat16 or wider, within the bound.
A program may use at most 128 MiB of HBM per device.

```python
import jax
import jax.numpy as jnp
from jax import lax

D = 4096
FF = 14336
EXPERTS = 8
TOP = 2
BLK = 128
GROUP = 8
TOKENS = 64
ROUTED = 2
HALF = 1
NB = 112
WORDS = 4
SLOTS = 120
COPIES = 8
EXP_WIN = 2


def route_table(key):
    key = jax.random.fold_in(key, 101)
    group_count = TOKENS // GROUP
    first_key, offset_key = jax.random.split(key)
    key_list = jax.random.split(first_key, group_count)
    orders = jax.vmap(lambda subkey: jax.random.permutation(subkey, GROUP))(key_list)
    leading = orders // (GROUP // EXPERTS)
    offset = jax.random.randint(offset_key, (group_count, 1), 1, EXPERTS)
    trailing = (leading + offset) % EXPERTS
    return jnp.stack([leading, trailing], axis=-1).reshape(TOKENS, 2).astype(jnp.int32)


def block_table(key):
    key = jax.random.fold_in(key, 202)
    order_key, place_key = jax.random.split(key)
    orders = jax.vmap(lambda subkey: jax.random.permutation(subkey, NB))(jax.random.split(order_key, EXPERTS))
    listing = jnp.concatenate([jnp.broadcast_to(jnp.arange(NB), (EXPERTS, NB)), orders[:, :COPIES]], axis=1)
    places = jax.vmap(lambda subkey: jax.random.permutation(subkey, SLOTS))(jax.random.split(place_key, EXPERTS))
    placed = jnp.take_along_axis(listing, places, axis=1)
    return (orders.astype(jnp.int32), placed.astype(jnp.int32))


def place_blocks(key, placed, factor):
    logical = jax.random.normal(key, (EXP_WIN, NB, BLK, D), jnp.float32) * factor
    slotted = jax.vmap(lambda blocks_all, slots_of: blocks_all[slots_of])(logical, placed)
    return slotted.reshape(EXP_WIN, SLOTS * BLK, D).astype(jnp.bfloat16)


def draw_routes(key, part):
    return route_table(key)


def draw_block_list(key, part):
    tables = block_table(key)
    return tables[1][:EXP_WIN]


def draw_gate_rows(key, part):
    tables = block_table(key)
    key = jax.random.fold_in(key, 7)
    return place_blocks(key, tables[1][:EXP_WIN], D ** (-0.5))


def draw_up_rows(key, part):
    tables = block_table(key)
    key = jax.random.fold_in(key, 8)
    return place_blocks(key, tables[1][:EXP_WIN], D ** (-0.5))


def draw_down_rows(key, part):
    tables = block_table(key)
    key = jax.random.fold_in(key, 9)
    return place_blocks(key, tables[1][:EXP_WIN], (FF // 8) ** (-0.5))


def draw_block_masks(key, part):
    routes = route_table(key)
    tables = block_table(key)
    orders = tables[0]
    key = jax.random.fold_in(key, 5)
    group_count = TOKENS // GROUP
    is_named = jnp.sum((routes[:, :, None] == jnp.arange(EXPERTS)[None, None, :]).astype(jnp.int32), axis=1)
    is_named = is_named.reshape(group_count, GROUP, EXPERTS)
    hot_flag = jnp.sum((jnp.arange(NB)[None, None, :] == orders[:, :COPIES, None]).astype(jnp.int32), axis=1)
    scores = jax.random.randint(key, (group_count, GROUP, EXPERTS, NB), 0, 2 ** 20) * GROUP
    scores = scores + jnp.arange(GROUP).astype(jnp.int32)[None, :, None, None]
    scores = jnp.where(is_named[..., None] == 1, scores, scores + 2 ** 20 * GROUP)
    ordering = jnp.argsort(scores, axis=1, stable=True)
    row_rank = jnp.argsort(ordering, axis=1, stable=True)
    cold_bits = is_named[..., None] * (row_rank < HALF).astype(jnp.int32)
    active = jnp.where(hot_flag[None, None, :, :] == 1, is_named[..., None], cold_bits)
    active = active.reshape(TOKENS, EXPERTS, NB)
    per_route = jnp.take_along_axis(active, routes[:, :, None], axis=1)
    padded = jnp.pad(per_route, ((0, 0), (0, 0), (0, WORDS * 30 - NB))).reshape(TOKENS, 2, WORDS, 30)
    powers = (2 ** jnp.arange(30)).astype(jnp.int32)
    return jnp.sum(padded * powers, axis=-1).astype(jnp.int32)


def plant(drawn, stream_key, least, top_value):
    place = [jax.random.randint(jax.random.fold_in(stream_key, axis), (), 0, length) for axis, length in enumerate(drawn.shape)]
    main_axis = drawn.shape.index(max(drawn.shape))
    beside = place[:main_axis] + [(place[main_axis] + 1) % drawn.shape[main_axis]] + place[main_axis + 1:]
    return drawn.at[tuple(place)].set(least).at[tuple(beside)].set(top_value)


def levels(stream_key, shape, cuts, low, largest):
    loudness = 1.0
    for axis_at, parts in cuts:
        draws = jax.random.uniform(jax.random.fold_in(jax.random.fold_in(stream_key, 6), axis_at), (parts,), jnp.float32, low / len(cuts), largest / len(cuts))
        loudness = loudness * jnp.repeat(jnp.exp(draws), shape[axis_at] // parts).reshape((-1,) + (1,) * (len(shape) - 1 - axis_at))
    return loudness


def bell_draw(rng, shape, deviation, most, cuts=(), held_as=jnp.bfloat16):
    drawn = deviation * jax.random.normal(rng, shape, jnp.float32)
    if cuts:
        drawn = drawn * levels(rng, shape, cuts, -0.22, 0.18)
    return jnp.clip(drawn, -most, most).astype(held_as)


def setup_inputs(seed: int = 0, part: int = 0) -> dict:
    seeds = jax.random.split(jax.random.key(seed), 9)
    own_keys = jax.random.split(jax.random.fold_in(seeds[8], part), 9)
    tokens = bell_draw(own_keys[0], (TOKENS, D), 1.0, 6.0, ((0, 16),))
    routes = draw_routes(jax.random.fold_in(jax.random.fold_in(seeds[8], part), 71), part)
    route_weights = plant(jax.random.randint(own_keys[2], (TOKENS, TOP), 6554, 65536), jax.random.fold_in(own_keys[2], 1), 6554, 65535).astype(jnp.int32)
    block_masks = draw_block_masks(jax.random.fold_in(jax.random.fold_in(seeds[8], part), 71), part)
    block_list = draw_block_list(jax.random.fold_in(jax.random.fold_in(seeds[8], part), 71), part)
    gate_rows = draw_gate_rows(jax.random.fold_in(jax.random.fold_in(seeds[8], part), 71), part)
    up_rows = draw_up_rows(jax.random.fold_in(jax.random.fold_in(seeds[8], part), 71), part)
    down_rows = draw_down_rows(jax.random.fold_in(jax.random.fold_in(seeds[8], part), 71), part)
    return dict(tokens=tokens, routes=routes, route_weights=route_weights, block_masks=block_masks, block_list=block_list, gate_rows=gate_rows, up_rows=up_rows, down_rows=down_rows)


def mask_bits(mask_words, block_ids):
    shifted = jnp.right_shift(jnp.take(mask_words, block_ids // 30, axis=-1), block_ids % 30)
    return jnp.bitwise_and(shifted, 1)


def reference(tokens, routes, route_weights, block_masks, block_list, gate_rows, up_rows, down_rows):
    block_count = FF // BLK
    slot_count = block_list.shape[1]
    slot_order = jnp.arange(slot_count).astype(jnp.int32)
    block_ids = jnp.arange(block_count).astype(jnp.int32)
    picked_count = TOKENS * ROUTED // GROUP
    summed = jnp.zeros((TOKENS, D), jnp.float32)
    for expert in range(EXP_WIN):
        is_named = (routes == expert).astype(jnp.int32)
        chosen = jnp.sum(is_named, axis=1)
        scaled = jnp.sum(is_named * route_weights, axis=1).astype(jnp.float32) / 65536.0
        mask_words = jnp.sum(is_named[:, :, None] * block_masks, axis=1)
        row_index = jnp.argsort(1 - chosen, stable=True)[:picked_count].astype(jnp.int32)
        row_block = tokens[row_index]
        alive = mask_bits(mask_words[row_index], block_ids).astype(jnp.float32)
        first_slot = jnp.min(jnp.where(block_list[expert][None, :] == block_ids[:, None], slot_order[None, :], slot_count), axis=1).astype(jnp.int32)
        gate_expert = gate_rows[expert]
        up_expert = up_rows[expert]
        down_expert = down_rows[expert]

        def add_block(running, element):
            slot_now, live_rows = element
            offset = (slot_now * BLK).astype(jnp.int32)
            gate_block = lax.dynamic_slice_in_dim(gate_expert, offset, BLK, 0)
            up_block = lax.dynamic_slice_in_dim(up_expert, offset, BLK, 0)
            down_block = lax.dynamic_slice_in_dim(down_expert, offset, BLK, 0)
            gate_pre = jnp.dot(row_block, gate_block.T, preferred_element_type=jnp.float32)
            up_pre = jnp.dot(row_block, up_block.T, preferred_element_type=jnp.float32)
            hidden = (jnp.maximum(gate_pre, 0.0) * jnp.maximum(up_pre, 0.0) * live_rows[:, None]).astype(jnp.bfloat16)
            return running + jnp.dot(hidden, down_block, preferred_element_type=jnp.float32), None

        outcome = lax.scan(add_block, jnp.zeros((picked_count, D), jnp.float32), (first_slot, alive.T))
        summed = summed.at[row_index].add(outcome[0] * scaled[row_index][:, None])
    return summed.astype(jnp.bfloat16)
```

```python
import functools

import jax
import jax.numpy as jnp
from jax import lax
from jax.experimental import pallas as pl
from jax.experimental.pallas import tpu as pltpu
from jax.sharding import PartitionSpec as P

BLK = 128
LANES = 128
UNITS = 4
F32 = jnp.float32
BF16 = jnp.bfloat16
MESH = pl.DeviceIdType.MESH


def total(value, axis):
    return jnp.sum(value, axis=axis, keepdims=True)


def picks_of(expert, routes, per_dev):
    low, high = None, None
    for half in range(2):
        named = jnp.max((routes[half] == expert).astype(F32), axis=1, keepdims=True)
        place = lax.broadcasted_iota(jnp.int32, (per_dev, 1), 0).astype(F32) + float(half * per_dev)
        least = jnp.min(jnp.where(named > 0.5, place, 1e6), axis=0, keepdims=True)
        most = jnp.max(jnp.where(named > 0.5, place, -1.0), axis=0, keepdims=True)
        low = least if low is None else jnp.minimum(low, least)
        high = most if high is None else jnp.maximum(high, most)
    return low, high


def kernel(
    neurons, chunk_slots,
    tok_in, routes_in, weights_in, masks_in, list_in, gate_hbm, up_hbm, down_hbm,
    out_ref,
    gate_v, up_v, down_v, pair_tok, pair_routes, pair_weights, pair_masks, slabs, lhs, bits_s,
    act, hid, acc, snd, rcv, rows_own, rows_other,
    gate_sem, up_sem, down_sem, pair_send, pair_recv, tok_send, tok_recv,
    out_send, out_recv, fin_send, fin_recv,
):
    me = lax.axis_index("neuron")
    expert = lax.axis_index("expert")
    other = 1 - expert
    per_dev, width = tok_in.shape
    subs = width // LANES
    unit = width // UNITS
    usubs = unit // LANES
    slots = gate_v.shape[0] // BLK
    rows = 2 * neurons
    chunk = chunk_slots * BLK
    chunks = slots // chunk_slots
    slab_rows = 2 * subs

    def weight_copy(hbm, vmem, sems, index):
        here = pl.ds(pl.multiple_of(index * chunk, chunk), chunk)
        return pltpu.make_async_copy(hbm.at[0, here, :], vmem.at[here, :], sems.at[index])

    def down_copy(index):
        return pltpu.make_async_copy(
            down_hbm.at[0, :, pl.ds(index * unit, unit)], down_v.at[index], down_sem.at[index]
        )

    for index in range(chunks):
        weight_copy(gate_hbm, gate_v, gate_sem, index).start()
        weight_copy(up_hbm, up_v, up_sem, index).start()
    for index in range(UNITS):
        down_copy(index).start()

    barrier = pltpu.get_barrier_semaphore()

    def greet(step, carry):
        pl.semaphore_signal(
            barrier, inc=1, device_id={"neuron": lax.rem(me + step, neurons)}, device_id_type=MESH
        )
        return carry

    pl.semaphore_signal(barrier, inc=1, device_id={"expert": other}, device_id_type=MESH)
    lax.fori_loop(1, neurons, greet, 0)

    pair_tok[expert] = tok_in[...].astype(F32).reshape(per_dev, subs, LANES).astype(BF16)
    pair_routes[expert] = routes_in[...]
    pair_weights[expert] = weights_in[...]
    pair_masks[expert] = masks_in[...]

    pl.semaphore_wait(barrier, neurons)

    def pair_copy(buffer, index):
        return pltpu.make_async_remote_copy(
            src_ref=buffer.at[expert], dst_ref=buffer.at[expert],
            send_sem=pair_send.at[index], recv_sem=pair_recv.at[index],
            device_id={"expert": other}, device_id_type=MESH,
        )

    pair_buffers = (pair_tok, pair_routes, pair_weights, pair_masks)
    for index, buffer in enumerate(pair_buffers):
        pair_copy(buffer, index).start()

    listed = list_in[...]
    slot_count = listed.shape[1]
    block_id = lax.broadcasted_iota(jnp.int32, (LANES, slot_count), 0)
    slot_id = lax.broadcasted_iota(jnp.int32, (LANES, slot_count), 1).astype(F32)
    first_slot = jnp.min(jnp.where(listed == block_id, slot_id, 1e6), axis=1, keepdims=True)
    own_slot = (lax.broadcasted_iota(jnp.int32, (LANES, LANES), 1) + me * slots).astype(F32)
    slot_lane = lax.broadcasted_iota(jnp.int32, (LANES, LANES), 1)
    holds = ((own_slot == first_slot) & (slot_lane < slots)).astype(F32).astype(BF16)

    for index, buffer in enumerate(pair_buffers):
        pair_copy(buffer, index).wait()

    routes = [pair_routes[half] for half in range(2)]
    picks = picks_of(expert, routes, per_dev)
    picks_other = picks_of(other, routes, per_dev)
    lane = lax.broadcasted_iota(jnp.int32, (1, LANES), 1)
    word_of = sum((lane >= 30 * word).astype(jnp.int32) for word in (1, 2, 3))
    shift = jnp.minimum(lane - 30 * word_of, 30)
    scales, bit_rows = [], []
    for pick in picks:
        scale, words = None, None
        for half in range(2):
            place = lax.broadcasted_iota(jnp.int32, (per_dev, 1), 0).astype(F32) + float(half * per_dev)
            for route in range(2):
                is_it = (routes[half][:, route:route + 1] == expert) & (place == pick)
                weight = total(jnp.where(is_it, pair_weights[half][:, route:route + 1].astype(F32), 0.0), 0)
                word = total(jnp.where(is_it, pair_masks[half, :, route, :], 0), 0)
                scale = weight if scale is None else scale + weight
                words = word if words is None else words + word
        scales.append(scale / 65536.0)
        spread = jnp.where(
            word_of == 0, words[:, 0:1],
            jnp.where(word_of == 1, words[:, 1:2], jnp.where(word_of == 2, words[:, 2:3], words[:, 3:4])),
        )
        bit_rows.append(jnp.bitwise_and(jnp.right_shift(spread, shift), 1).astype(F32))

    for row, pick in enumerate(picks):
        chosen = jnp.zeros((subs, LANES), F32)
        for token in range(2 * per_dev):
            gain = (pick == float(token)).astype(F32)
            chosen = chosen + gain * pair_tok[token // per_dev, token % per_dev].astype(F32)
        slabs[me, row * subs:(row + 1) * subs, :] = chosen.astype(BF16)
    line = lax.broadcasted_iota(jnp.int32, (16, LANES), 0)
    slabs[me, slab_rows:slab_rows + 16, :] = jnp.where(
        line == 0, bit_rows[0], jnp.where(line == 1, bit_rows[1], 0.0)
    ).astype(BF16)

    def token_copy(step, source):
        return pltpu.make_async_remote_copy(
            src_ref=slabs.at[source], dst_ref=slabs.at[source],
            send_sem=tok_send.at[step], recv_sem=tok_recv.at[source],
            device_id={"neuron": lax.rem(me + step, neurons)}, device_id_type=MESH,
        )

    def token_start(step, carry):
        token_copy(step, me).start()
        return carry

    def token_arrive(step, carry):
        token_copy(step, lax.rem(me + step, neurons)).wait_recv()
        return carry

    def token_leave(step, carry):
        token_copy(step, me).wait_send()
        return carry

    lax.fori_loop(1, neurons, token_start, 0)
    lax.fori_loop(1, neurons, token_arrive, 0)

    def unpack(part, carry):
        arrived = slabs[pl.ds(part * 8, 8), 0:slab_rows, :].astype(F32)
        lhs[pl.ds(pl.multiple_of(part * 16, 16), 16), :] = arrived.reshape(16, subs, LANES).reshape(16, width).astype(BF16)
        return carry

    lax.fori_loop(0, neurons // 8, unpack, 0)
    for source in range(neurons):
        bits_s[2 * source:2 * source + 2, :] = slabs[source, slab_rows:slab_rows + 16, :].astype(F32)[0:2, :]
    active = jnp.dot(bits_s[...].astype(BF16), holds, preferred_element_type=F32)
    for slot in range(slots):
        act[:, slot * BLK:(slot + 1) * BLK] = jnp.broadcast_to(active[:, slot:slot + 1], (rows, BLK))

    def hidden_chunk(index, carry):
        here = pl.ds(pl.multiple_of(index * chunk, chunk), chunk)
        weight_copy(gate_hbm, gate_v, gate_sem, index).wait()
        weight_copy(up_hbm, up_v, up_sem, index).wait()
        contract = (((1,), (1,)), ((), ()))
        gate_pre = lax.dot_general(lhs[...], gate_v[here, :], contract, preferred_element_type=F32)
        up_pre = lax.dot_general(lhs[...], up_v[here, :], contract, preferred_element_type=F32)
        product = jnp.maximum(gate_pre, 0.0) * jnp.maximum(up_pre, 0.0)
        hid[:, here] = (product * act[:, here]).astype(BF16)
        return carry

    lax.fori_loop(0, chunks, hidden_chunk, 0)
    lax.fori_loop(1, neurons, token_leave, 0)

    def out_copy(index, step, row, slot):
        return pltpu.make_async_remote_copy(
            src_ref=snd.at[index, row], dst_ref=rcv.at[index, slot],
            send_sem=out_send.at[index, step], recv_sem=out_recv.at[index, slot],
            device_id={"neuron": lax.rem(me + step, neurons)}, device_id_type=MESH,
        )

    def down_unit(index, carry):
        down_copy(index).wait()
        acc[...] = jnp.dot(hid[...], down_v[index], preferred_element_type=F32)

        def pack(part, inner):
            partial = acc[pl.ds(pl.multiple_of(part * 16, 16), 16), :]
            packed = partial.reshape(16, usubs, LANES).reshape(8, 2 * usubs, LANES)
            snd[index, pl.ds(part * 8, 8)] = packed.astype(BF16)
            return inner

        lax.fori_loop(0, neurons // 8, pack, 0)
        rcv[index, me] = snd[index, me]

        def send(step, inner):
            out_copy(index, step, lax.rem(me + step, neurons), me).start()
            return inner

        lax.fori_loop(1, neurons, send, 0)
        return carry

    lax.fori_loop(0, UNITS, down_unit, 0)

    def fin_copy(index):
        return pltpu.make_async_remote_copy(
            src_ref=rows_own.at[index], dst_ref=rows_other.at[index],
            send_sem=fin_send.at[index], recv_sem=fin_recv.at[index],
            device_id={"expert": other}, device_id_type=MESH,
        )

    upper = lax.broadcasted_iota(jnp.int32, (2 * usubs, LANES), 0) < usubs
    scale_rows = jnp.where(upper, scales[0], scales[1])

    def collect(index, carry):
        def arrive(step, inner):
            source = lax.rem(me + step, neurons)
            out_copy(index, step, source, source).wait_recv()
            return inner

        lax.fori_loop(1, neurons, arrive, 0)
        summed = jnp.sum(rcv[index].astype(F32), axis=0)
        rows_own[index] = summed * scale_rows
        fin_copy(index).start()
        return carry

    lax.fori_loop(0, UNITS, collect, 0)

    offset = (expert * per_dev).astype(F32)
    for index in range(UNITS):
        fin_copy(index).wait_recv()
        mine, others = rows_own[index], rows_other[index]
        tokens_out = []
        for token in range(per_dev):
            place = offset + float(token)
            value = jnp.zeros((usubs, LANES), F32)
            for source, pick_pair in ((mine, picks), (others, picks_other)):
                for row in range(2):
                    gain = (pick_pair[row] == place).astype(F32)
                    value = value + gain * source[row * usubs:(row + 1) * usubs, :]
            tokens_out.append(value[None])
        stacked = jnp.concatenate(tokens_out, axis=0).reshape(per_dev, unit)
        out_ref[:, index * unit:(index + 1) * unit] = stacked.astype(BF16)

    for index in range(UNITS):
        fin_copy(index).wait_send()

    def drain(index, carry):
        def leave(step, inner):
            out_copy(index, step, lax.rem(me + step, neurons), me).wait_send()
            return inner

        return lax.fori_loop(1, neurons, leave, carry)

    lax.fori_loop(0, UNITS, drain, 0)


def local(tokens, routes, route_weights, block_masks, block_list, gate_rows, up_rows, down_rows):
    neurons = lax.axis_size("neuron")
    per_dev, width = tokens.shape
    held = gate_rows.shape[1]
    slots = held // BLK
    chunk_slots = max(size for size in (1, 2, 3) if slots % size == 0)
    chunks = slots // chunk_slots
    rows = 2 * neurons
    subs = width // LANES
    unit = width // UNITS
    usubs = unit // LANES
    vmem = pl.BlockSpec(memory_space=pltpu.VMEM)
    hbm = pl.BlockSpec(memory_space=pl.ANY)
    dma = pltpu.SemaphoreType.DMA
    return pl.pallas_call(
        functools.partial(kernel, neurons, chunk_slots),
        out_shape=jax.ShapeDtypeStruct((per_dev, width), BF16),
        in_specs=[vmem] * 5 + [hbm] * 3,
        out_specs=vmem,
        scratch_shapes=[
            pltpu.VMEM((held, width), BF16),
            pltpu.VMEM((held, width), BF16),
            pltpu.VMEM((UNITS, held, unit), BF16),
            pltpu.VMEM((2, per_dev, subs, LANES), BF16),
            pltpu.VMEM((2,) + routes.shape, jnp.int32),
            pltpu.VMEM((2,) + route_weights.shape, jnp.int32),
            pltpu.VMEM((2,) + block_masks.shape, jnp.int32),
            pltpu.VMEM((neurons, 2 * subs + 16, LANES), BF16),
            pltpu.VMEM((rows, width), BF16),
            pltpu.VMEM((rows, LANES), F32),
            pltpu.VMEM((rows, held), F32),
            pltpu.VMEM((rows, held), BF16),
            pltpu.VMEM((rows, unit), F32),
            pltpu.VMEM((UNITS, neurons, 2 * usubs, LANES), BF16),
            pltpu.VMEM((UNITS, neurons, 2 * usubs, LANES), BF16),
            pltpu.VMEM((UNITS, 2 * usubs, LANES), F32),
            pltpu.VMEM((UNITS, 2 * usubs, LANES), F32),
            dma((chunks,)),
            dma((chunks,)),
            dma((UNITS,)),
            dma((4,)),
            dma((4,)),
            dma((neurons,)),
            dma((neurons,)),
            dma((UNITS, neurons)),
            dma((UNITS, neurons)),
            dma((UNITS,)),
            dma((UNITS,)),
        ],
        compiler_params=pltpu.CompilerParams(
            collective_id=0, has_side_effects=True, vmem_limit_bytes=58 * 1024 * 1024
        ),
    )(tokens, routes, route_weights, block_masks, block_list, gate_rows, up_rows, down_rows)


def solution(mesh):
    placed = (
        P(("groups", "neuron", "expert"), None),
        P(("groups", "neuron", "expert"), None),
        P(("groups", "neuron", "expert"), None),
        P(("groups", "neuron", "expert"), None, None),
        P(("groups", "expert"), None),
        P(("groups", "expert"), "neuron", None),
        P(("groups", "expert"), "neuron", None),
        P(("groups", "expert"), "neuron", None),
    )
    return jax.shard_map(
        local,
        mesh=mesh,
        in_specs=placed,
        out_specs=P(("groups", "neuron", "expert"), None),
        check_vma=False,
    )
```

```python
import functools

import jax
import jax.numpy as jnp
from jax import lax
from jax.experimental import pallas as pl
from jax.experimental.pallas import tpu as pltpu
from jax.sharding import PartitionSpec as P

BLK = 128
LANES = 128
UNITS = 4
PARTS = 2
F32 = jnp.float32
BF16 = jnp.bfloat16
MESH = pl.DeviceIdType.MESH


def total(value, axis):
    return jnp.sum(value, axis=axis, keepdims=True)


def picks_of(expert, routes, places):
    low, high = None, None
    for half in range(2):
        named = jnp.max((routes[half] == expert).astype(F32), axis=0, keepdims=True)
        least = jnp.min(jnp.where(named > 0.5, places[half], 1e6), axis=1, keepdims=True)
        most = jnp.max(jnp.where(named > 0.5, places[half], -1.0), axis=1, keepdims=True)
        low = least if low is None else jnp.minimum(low, least)
        high = most if high is None else jnp.maximum(high, most)
    return low, high


def kernel(
    neurons, group_slots,
    tok_in, routes_in, weights_in, masks_in, list_in, gate_hbm, up_hbm, down_hbm,
    out_ref,
    both_v, down_v, tok_v, list_v, pair_tok, pair_routes, pair_weights, pair_masks, slabs, slab_bits, lhs, bits_s,
    act, pre, hid, acc, snd, rcv, rows_own, rows_other,
    both_sem, down_sem, in_sem, pair_send, pair_recv, tok_send, tok_recv,
    out_send, out_recv, fin_send, fin_recv,
):
    me = lax.axis_index("neuron")
    expert = lax.axis_index("expert")
    other = 1 - expert
    per_dev, width = tok_in.shape
    subs = width // LANES
    part_width = width // PARTS
    part_subs = subs // PARTS
    unit = width // UNITS
    usubs = unit // LANES
    slots = both_v.shape[1]
    rows = 2 * neurons
    groups = slots // group_slots
    few = neurons <= 8

    barrier = pltpu.get_barrier_semaphore()

    def greet(step, carry):
        pl.semaphore_signal(
            barrier, inc=1, device_id={"neuron": lax.rem(me + step, neurons)}, device_id_type=MESH
        )
        return carry

    pl.semaphore_signal(barrier, inc=1, device_id={"expert": other}, device_id_type=MESH)
    lax.fori_loop(1, neurons, greet, 0, unroll=few)

    def small_copies():
        pairs = (
            (tok_in, tok_v), (routes_in, pair_routes.at[expert]), (weights_in, pair_weights.at[expert]),
            (masks_in, pair_masks.at[expert]), (list_in, list_v),
        )
        return [pltpu.make_async_copy(src, dst, in_sem.at[at]) for at, (src, dst) in enumerate(pairs)]

    for copy in small_copies():
        copy.start()

    def both_copies(part, slot):
        columns = pl.ds(part * part_width, part_width)
        here = pl.ds(pl.multiple_of(slot * BLK, BLK), BLK)
        return [
            pltpu.make_async_copy(
                hbm.at[0, here, columns], both_v.at[part, slot, pl.ds(side * BLK, BLK), :],
                both_sem.at[part, slot, side],
            )
            for side, hbm in enumerate((gate_hbm, up_hbm))
        ]

    def down_copy(index):
        return pltpu.make_async_copy(
            down_hbm.at[0, :, pl.ds(index * unit, unit)], down_v.at[index], down_sem.at[index]
        )

    for part in range(PARTS):
        def begin(slot, carry, part=part):
            for copy in both_copies(part, slot):
                copy.start()
            return carry

        lax.fori_loop(0, slots, begin, 0)
    for index in range(UNITS):
        down_copy(index).start()

    for copy in small_copies():
        copy.wait()
    pair_tok[expert] = tok_v[...].astype(F32).reshape(per_dev, subs, LANES).astype(BF16)

    pl.semaphore_wait(barrier, neurons)

    def pair_copy(buffer, index):
        return pltpu.make_async_remote_copy(
            src_ref=buffer.at[expert], dst_ref=buffer.at[expert],
            send_sem=pair_send.at[index], recv_sem=pair_recv.at[index],
            device_id={"expert": other}, device_id_type=MESH,
        )

    pair_buffers = (pair_tok, pair_routes, pair_weights, pair_masks)
    for index, buffer in enumerate(pair_buffers):
        pair_copy(buffer, index).start()

    listed = list_v[...]
    slot_count = listed.shape[1]
    block_id = lax.broadcasted_iota(jnp.int32, (LANES, slot_count), 0)
    slot_id = lax.broadcasted_iota(jnp.int32, (LANES, slot_count), 1).astype(F32)
    first_slot = jnp.min(jnp.where(listed == block_id, slot_id, 1e6), axis=1, keepdims=True)
    own_slot = (lax.broadcasted_iota(jnp.int32, (LANES, LANES), 1) + me * slots).astype(F32)
    slot_lane = lax.broadcasted_iota(jnp.int32, (LANES, LANES), 1)
    holds = ((own_slot == first_slot) & (slot_lane < slots)).astype(F32).astype(BF16)

    for index, buffer in enumerate(pair_buffers):
        pair_copy(buffer, index).wait()

    routes = [pair_routes[half] for half in range(2)]
    places = [
        lax.broadcasted_iota(jnp.int32, (1, per_dev), 1).astype(F32) + float(half * per_dev) for half in range(2)
    ]
    picks = picks_of(expert, routes, places)
    picks_other = picks_of(other, routes, places)

    def token_copy(part, step, source):
        buffer = slabs.at[part, source] if part < PARTS else slab_bits.at[source]
        return pltpu.make_async_remote_copy(
            src_ref=buffer, dst_ref=buffer,
            send_sem=tok_send.at[part, step], recv_sem=tok_recv.at[part, source],
            device_id={"neuron": lax.rem(me + step, neurons)}, device_id_type=MESH,
        )

    def token_start(part):
        def start(step, carry):
            token_copy(part, step, me).start()
            return carry

        lax.fori_loop(1, neurons, start, 0, unroll=few)

    def token_arrive(part):
        def arrive(step, carry):
            token_copy(part, step, lax.rem(me + step, neurons)).wait_recv()
            return carry

        lax.fori_loop(1, neurons, arrive, 0, unroll=few)

    gains = [[(pick == float(token)).astype(F32) for token in range(2 * per_dev)] for pick in picks]
    for part in range(PARTS):
        here = slice(part * part_subs, (part + 1) * part_subs)
        for row in range(2):
            chosen = jnp.zeros((part_subs, LANES), F32)
            for token in range(2 * per_dev):
                chosen = chosen + gains[row][token] * pair_tok[token // per_dev, token % per_dev, here, :].astype(F32)
            slabs[part, me, row * part_subs:(row + 1) * part_subs, :] = chosen.astype(BF16)
        token_start(part)

    lane = lax.broadcasted_iota(jnp.int32, (1, LANES), 1)
    word_of = sum((lane >= 30 * word).astype(jnp.int32) for word in (1, 2, 3))
    shift = jnp.minimum(lane - 30 * word_of, 30)
    scales, bit_rows = [], []
    for row, pick in enumerate(picks):
        scale, words = None, None
        for half in range(2):
            is_it = (routes[half] == expert) & (places[half] == pick)
            weight = total(total(jnp.where(is_it, pair_weights[half].astype(F32), 0.0), 0), 1)
            scale = weight if scale is None else scale + weight
            for token in range(per_dev):
                named = (routes[half][:, token:token + 1] == expert) & (gains[row][half * per_dev + token] > 0.5)
                word = jnp.where(named, pair_masks[half, token], 0)
                words = word if words is None else words + word
        words = total(words, 0)
        scales.append(scale / 65536.0)
        spread = jnp.where(
            word_of == 0, words[:, 0:1],
            jnp.where(word_of == 1, words[:, 1:2], jnp.where(word_of == 2, words[:, 2:3], words[:, 3:4])),
        )
        bit_rows.append(jnp.bitwise_and(jnp.right_shift(spread, shift), 1).astype(F32))
    line = lax.broadcasted_iota(jnp.int32, (16, LANES), 0)
    slab_bits[me] = jnp.where(line == 0, bit_rows[0], jnp.where(line == 1, bit_rows[1], 0.0)).astype(BF16)
    token_start(PARTS)

    def unpack(part):
        def piece(at, carry):
            arrived = slabs[part, pl.ds(at * 8, 8)].astype(F32)
            lhs[part, pl.ds(pl.multiple_of(at * 16, 16), 16), :] = (
                arrived.reshape(16, part_subs, LANES).reshape(16, part_width).astype(BF16)
            )
            return carry

        lax.fori_loop(0, neurons // 8, piece, 0)

    contract = (((1,), (1,)), ((), ()))
    for part in range(PARTS):
        token_arrive(part)
        unpack(part)
        last = part == PARTS - 1
        if last:
            token_arrive(PARTS)
            for source in range(neurons):
                bits_s[2 * source:2 * source + 2, :] = slab_bits[source].astype(F32)[0:2, :]
            active = jnp.dot(bits_s[...].astype(BF16), holds, preferred_element_type=F32)
            for slot in range(slots):
                act[slot] = jnp.broadcast_to(active[:, slot:slot + 1], (rows, BLK))

        def multiply(group, carry, part=part, last=last):
            for inner in range(group_slots):
                for copy in both_copies(part, group * group_slots + inner):
                    copy.wait()
            for inner in range(group_slots):
                slot = group * group_slots + inner
                value = lax.dot_general(lhs[part], both_v[part, slot], contract, preferred_element_type=F32)
                if part > 0:
                    value = value + pre[slot]
                if last:
                    product = jnp.maximum(value[:, :BLK], 0.0) * jnp.maximum(value[:, BLK:], 0.0)
                    hid[:, pl.ds(pl.multiple_of(slot * BLK, BLK), BLK)] = (product * act[slot]).astype(BF16)
                else:
                    pre[slot] = value
            return carry

        lax.fori_loop(0, groups, multiply, 0)

    def out_copy(index, step, row, slot):
        return pltpu.make_async_remote_copy(
            src_ref=snd.at[index, row], dst_ref=rcv.at[index, slot],
            send_sem=out_send.at[index, step], recv_sem=out_recv.at[index, slot],
            device_id={"neuron": lax.rem(me + step, neurons)}, device_id_type=MESH,
        )

    def down_unit(index, carry):
        down_copy(index).wait()
        acc[...] = jnp.dot(hid[...], down_v[index], preferred_element_type=F32)

        def pack(part, inner):
            partial = acc[pl.ds(pl.multiple_of(part * 16, 16), 16), :]
            packed = partial.reshape(16, usubs, LANES).reshape(8, 2 * usubs, LANES)
            snd[index, pl.ds(part * 8, 8)] = packed.astype(BF16)
            return inner

        lax.fori_loop(0, neurons // 8, pack, 0)
        rcv[index, me] = snd[index, me]

        def send(step, inner):
            out_copy(index, step, lax.rem(me + step, neurons), me).start()
            return inner

        lax.fori_loop(1, neurons, send, 0, unroll=few)
        return carry

    lax.fori_loop(0, UNITS, down_unit, 0)

    def fin_copy(index):
        return pltpu.make_async_remote_copy(
            src_ref=rows_own.at[index], dst_ref=rows_other.at[index],
            send_sem=fin_send.at[index], recv_sem=fin_recv.at[index],
            device_id={"expert": other}, device_id_type=MESH,
        )

    upper = lax.broadcasted_iota(jnp.int32, (2 * usubs, LANES), 0) < usubs
    scale_rows = jnp.where(upper, scales[0], scales[1])

    def collect(index, carry):
        def arrive(step, inner):
            source = lax.rem(me + step, neurons)
            out_copy(index, step, source, source).wait_recv()
            return inner

        lax.fori_loop(1, neurons, arrive, 0, unroll=few)
        summed = jnp.sum(rcv[index].astype(F32), axis=0)
        rows_own[index] = summed * scale_rows
        fin_copy(index).start()
        return carry

    lax.fori_loop(0, UNITS, collect, 0)

    offset = (expert * per_dev).astype(F32)
    for index in range(UNITS):
        fin_copy(index).wait_recv()
        mine, others = rows_own[index], rows_other[index]
        tokens_out = []
        for token in range(per_dev):
            place = offset + float(token)
            value = jnp.zeros((usubs, LANES), F32)
            for source, pick_pair in ((mine, picks), (others, picks_other)):
                for row in range(2):
                    gain = (pick_pair[row] == place).astype(F32)
                    value = value + gain * source[row * usubs:(row + 1) * usubs, :]
            tokens_out.append(value[None])
        stacked = jnp.concatenate(tokens_out, axis=0).reshape(per_dev, unit)
        out_ref[:, index * unit:(index + 1) * unit] = stacked.astype(BF16)

    for index in range(UNITS):
        fin_copy(index).wait_send()

    def drain(index, carry):
        def leave(step, inner):
            out_copy(index, step, lax.rem(me + step, neurons), me).wait_send()
            return inner

        return lax.fori_loop(1, neurons, leave, carry, unroll=few)

    lax.fori_loop(0, UNITS, drain, 0)
    for part in range(PARTS + 1):
        def leave_token(step, carry, part=part):
            token_copy(part, step, me).wait_send()
            return carry

        lax.fori_loop(1, neurons, leave_token, 0, unroll=few)


def local(tokens, routes, route_weights, block_masks, block_list, gate_rows, up_rows, down_rows):
    routes, route_weights = routes.T, route_weights.T
    neurons = lax.axis_size("neuron")
    per_dev, width = tokens.shape
    held = gate_rows.shape[1]
    slots = held // BLK
    group_slots = max(size for size in (1, 3, 5) if slots % size == 0)
    rows = 2 * neurons
    subs = width // LANES
    unit = width // UNITS
    usubs = unit // LANES
    part_width = width // PARTS
    vmem = pl.BlockSpec(memory_space=pltpu.VMEM)
    hbm = pl.BlockSpec(memory_space=pl.ANY)
    dma = pltpu.SemaphoreType.DMA
    return pl.pallas_call(
        functools.partial(kernel, neurons, group_slots),
        out_shape=jax.ShapeDtypeStruct((per_dev, width), BF16),
        in_specs=[hbm] * 8,
        out_specs=vmem,
        scratch_shapes=[
            pltpu.VMEM((PARTS, slots, 2 * BLK, part_width), BF16),
            pltpu.VMEM((UNITS, held, unit), BF16),
            pltpu.VMEM((per_dev, width), BF16),
            pltpu.VMEM(block_list.shape, jnp.int32),
            pltpu.VMEM((2, per_dev, subs, LANES), BF16),
            pltpu.VMEM((2,) + routes.shape, jnp.int32),
            pltpu.VMEM((2,) + route_weights.shape, jnp.int32),
            pltpu.VMEM((2,) + block_masks.shape, jnp.int32),
            pltpu.VMEM((PARTS, neurons, 2 * subs // PARTS, LANES), BF16),
            pltpu.VMEM((neurons, 16, LANES), BF16),
            pltpu.VMEM((PARTS, rows, part_width), BF16),
            pltpu.VMEM((rows, LANES), F32),
            pltpu.VMEM((slots, rows, BLK), F32),
            pltpu.VMEM((slots, rows, 2 * BLK), F32),
            pltpu.VMEM((rows, held), BF16),
            pltpu.VMEM((rows, unit), F32),
            pltpu.VMEM((UNITS, neurons, 2 * usubs, LANES), BF16),
            pltpu.VMEM((UNITS, neurons, 2 * usubs, LANES), BF16),
            pltpu.VMEM((UNITS, 2 * usubs, LANES), F32),
            pltpu.VMEM((UNITS, 2 * usubs, LANES), F32),
            dma((PARTS, slots, 2)),
            dma((UNITS,)),
            dma((5,)),
            dma((4,)),
            dma((4,)),
            dma((PARTS + 1, neurons)),
            dma((PARTS + 1, neurons)),
            dma((UNITS, neurons)),
            dma((UNITS, neurons)),
            dma((UNITS,)),
            dma((UNITS,)),
        ],
        compiler_params=pltpu.CompilerParams(
            collective_id=0, has_side_effects=True, vmem_limit_bytes=58 * 1024 * 1024
        ),
    )(tokens, routes, route_weights, block_masks, block_list, gate_rows, up_rows, down_rows)


def solution(mesh):
    placed = (
        P(("groups", "neuron", "expert"), None),
        P(("groups", "neuron", "expert"), None),
        P(("groups", "neuron", "expert"), None),
        P(("groups", "neuron", "expert"), None, None),
        P(("groups", "expert"), None),
        P(("groups", "expert"), "neuron", None),
        P(("groups", "expert"), "neuron", None),
        P(("groups", "expert"), "neuron", None),
    )
    return jax.shard_map(
        local,
        mesh=mesh,
        in_specs=placed,
        out_specs=P(("groups", "neuron", "expert"), None),
        check_vma=False,
    )
```

```python
import functools

import jax
import jax.numpy as jnp
from jax import lax
from jax.experimental import pallas as pl
from jax.experimental.pallas import tpu as pltpu
from jax.sharding import PartitionSpec as P

BLK = 128
LANES = 128
UNITS = 2
PARTS = 2
F32 = jnp.float32
BF16 = jnp.bfloat16
MESH = pl.DeviceIdType.MESH


def total(value, axis):
    return jnp.sum(value, axis=axis, keepdims=True)


def picks_of(expert, routes, places):
    low, high = None, None
    for half in range(2):
        named = jnp.max((routes[half] == expert).astype(F32), axis=0, keepdims=True)
        least = jnp.min(jnp.where(named > 0.5, places[half], 1e6), axis=1, keepdims=True)
        most = jnp.max(jnp.where(named > 0.5, places[half], -1.0), axis=1, keepdims=True)
        low = least if low is None else jnp.minimum(low, least)
        high = most if high is None else jnp.maximum(high, most)
    return low, high


def kernel(
    neurons, group_slots,
    tok_in, routes_in, weights_in, masks_in, list_in, gate_hbm, up_hbm, down_hbm,
    out_ref,
    both_v, down_v, tok_v, list_v, pair_tok, pair_routes, pair_weights, pair_masks, slabs, slab_bits, lhs, bits_s,
    act, pre, hid, acc, snd, rcv, rows_own, rows_other,
    both_sem, down_sem, in_sem, pair_send, pair_recv, tok_send, tok_recv,
    out_send, out_recv, fin_send, fin_recv,
):
    me = lax.axis_index("neuron")
    expert = lax.axis_index("expert")
    other = 1 - expert
    per_dev, width = tok_in.shape
    subs = width // LANES
    part_width = width // PARTS
    part_subs = subs // PARTS
    unit = width // UNITS
    usubs = unit // LANES
    slots = both_v.shape[1]
    rows = 2 * neurons
    groups = slots // group_slots
    few = neurons <= 8

    barrier = pltpu.get_barrier_semaphore()

    def greet(step, carry):
        pl.semaphore_signal(
            barrier, inc=1, device_id={"neuron": lax.rem(me + step, neurons)}, device_id_type=MESH
        )
        return carry

    pl.semaphore_signal(barrier, inc=1, device_id={"expert": other}, device_id_type=MESH)
    lax.fori_loop(1, neurons, greet, 0, unroll=few)

    def small_copies():
        pairs = (
            (tok_in, tok_v), (routes_in, pair_routes.at[expert]), (weights_in, pair_weights.at[expert]),
            (masks_in, pair_masks.at[expert]), (list_in, list_v),
        )
        return [pltpu.make_async_copy(src, dst, in_sem.at[at]) for at, (src, dst) in enumerate(pairs)]

    for copy in small_copies():
        copy.start()

    def both_copies(part, slot):
        columns = pl.ds(part * part_width, part_width)
        here = pl.ds(pl.multiple_of(slot * BLK, BLK), BLK)
        return [
            pltpu.make_async_copy(
                hbm.at[0, here, columns], both_v.at[part, slot, pl.ds(side * BLK, BLK), :],
                both_sem.at[part, slot, side],
            )
            for side, hbm in enumerate((gate_hbm, up_hbm))
        ]

    def down_copy(index):
        return pltpu.make_async_copy(
            down_hbm.at[0, :, pl.ds(index * unit, unit)], down_v.at[index], down_sem.at[index]
        )

    for part in range(PARTS):
        def begin(slot, carry, part=part):
            for copy in both_copies(part, slot):
                copy.start()
            return carry

        lax.fori_loop(0, slots, begin, 0)
    for index in range(UNITS):
        down_copy(index).start()

    for copy in small_copies():
        copy.wait()
    pair_tok[expert] = tok_v[...].astype(F32).reshape(per_dev, subs, LANES).astype(BF16)

    pl.semaphore_wait(barrier, neurons)

    def pair_copy(buffer, index):
        return pltpu.make_async_remote_copy(
            src_ref=buffer.at[expert], dst_ref=buffer.at[expert],
            send_sem=pair_send.at[index], recv_sem=pair_recv.at[index],
            device_id={"expert": other}, device_id_type=MESH,
        )

    pair_buffers = (pair_tok, pair_routes, pair_weights, pair_masks)
    for index, buffer in enumerate(pair_buffers):
        pair_copy(buffer, index).start()

    listed = list_v[...]
    slot_count = listed.shape[1]
    block_id = lax.broadcasted_iota(jnp.int32, (LANES, slot_count), 0)
    slot_id = lax.broadcasted_iota(jnp.int32, (LANES, slot_count), 1).astype(F32)
    first_slot = jnp.min(jnp.where(listed == block_id, slot_id, 1e6), axis=1, keepdims=True)
    own_slot = (lax.broadcasted_iota(jnp.int32, (LANES, LANES), 1) + me * slots).astype(F32)
    slot_lane = lax.broadcasted_iota(jnp.int32, (LANES, LANES), 1)
    holds = ((own_slot == first_slot) & (slot_lane < slots)).astype(F32).astype(BF16)

    for index, buffer in enumerate(pair_buffers):
        pair_copy(buffer, index).wait()

    routes = [pair_routes[half] for half in range(2)]
    places = [
        lax.broadcasted_iota(jnp.int32, (1, per_dev), 1).astype(F32) + float(half * per_dev) for half in range(2)
    ]
    picks = picks_of(expert, routes, places)
    picks_other = picks_of(other, routes, places)

    def token_copy(part, step, source):
        buffer = slabs.at[part, source] if part < PARTS else slab_bits.at[source]
        return pltpu.make_async_remote_copy(
            src_ref=buffer, dst_ref=buffer,
            send_sem=tok_send.at[part, step], recv_sem=tok_recv.at[part, source],
            device_id={"neuron": lax.rem(me + step, neurons)}, device_id_type=MESH,
        )

    def token_start(part):
        def start(step, carry):
            token_copy(part, step, me).start()
            return carry

        lax.fori_loop(1, neurons, start, 0, unroll=few)

    def token_arrive(part):
        def arrive(step, carry):
            token_copy(part, step, lax.rem(me + step, neurons)).wait_recv()
            return carry

        lax.fori_loop(1, neurons, arrive, 0, unroll=few)

    gains = [[(pick == float(token)).astype(F32) for token in range(2 * per_dev)] for pick in picks]
    for part in range(PARTS):
        here = slice(part * part_subs, (part + 1) * part_subs)
        for row in range(2):
            chosen = jnp.zeros((part_subs, LANES), F32)
            for token in range(2 * per_dev):
                chosen = chosen + gains[row][token] * pair_tok[token // per_dev, token % per_dev, here, :].astype(F32)
            slabs[part, me, row * part_subs:(row + 1) * part_subs, :] = chosen.astype(BF16)
        token_start(part)

    lane = lax.broadcasted_iota(jnp.int32, (1, LANES), 1)
    word_of = sum((lane >= 30 * word).astype(jnp.int32) for word in (1, 2, 3))
    shift = jnp.minimum(lane - 30 * word_of, 30)
    scales, bit_rows = [], []
    for row, pick in enumerate(picks):
        scale, words = None, None
        for half in range(2):
            is_it = (routes[half] == expert) & (places[half] == pick)
            weight = total(total(jnp.where(is_it, pair_weights[half].astype(F32), 0.0), 0), 1)
            scale = weight if scale is None else scale + weight
            for token in range(per_dev):
                named = (routes[half][:, token:token + 1] == expert) & (gains[row][half * per_dev + token] > 0.5)
                word = jnp.where(named, pair_masks[half, token], 0)
                words = word if words is None else words + word
        words = total(words, 0)
        scales.append(scale / 65536.0)
        spread = jnp.where(
            word_of == 0, words[:, 0:1],
            jnp.where(word_of == 1, words[:, 1:2], jnp.where(word_of == 2, words[:, 2:3], words[:, 3:4])),
        )
        bit_rows.append(jnp.bitwise_and(jnp.right_shift(spread, shift), 1).astype(F32))
    line = lax.broadcasted_iota(jnp.int32, (16, LANES), 0)
    slab_bits[me] = jnp.where(line == 0, bit_rows[0], jnp.where(line == 1, bit_rows[1], 0.0)).astype(BF16)
    token_start(PARTS)

    def unpack(part):
        def piece(at, carry):
            arrived = slabs[part, pl.ds(at * 8, 8)].astype(F32)
            lhs[part, pl.ds(pl.multiple_of(at * 16, 16), 16), :] = (
                arrived.reshape(16, part_subs, LANES).reshape(16, part_width).astype(BF16)
            )
            return carry

        lax.fori_loop(0, neurons // 8, piece, 0)

    contract = (((1,), (1,)), ((), ()))
    for part in range(PARTS):
        token_arrive(part)
        unpack(part)
        last = part == PARTS - 1
        if last:
            token_arrive(PARTS)
            for source in range(neurons):
                bits_s[2 * source:2 * source + 2, :] = slab_bits[source].astype(F32)[0:2, :]
            active = jnp.dot(bits_s[...].astype(BF16), holds, preferred_element_type=F32)
            for slot in range(slots):
                act[slot] = jnp.broadcast_to(active[:, slot:slot + 1], (rows, BLK))

        def multiply(group, carry, part=part, last=last):
            for inner in range(group_slots):
                for copy in both_copies(part, group * group_slots + inner):
                    copy.wait()
            for inner in range(group_slots):
                slot = group * group_slots + inner
                value = lax.dot_general(lhs[part], both_v[part, slot], contract, preferred_element_type=F32)
                if part > 0:
                    value = value + pre[slot]
                if last:
                    product = jnp.maximum(value[:, :BLK], 0.0) * jnp.maximum(value[:, BLK:], 0.0)
                    hid[:, pl.ds(pl.multiple_of(slot * BLK, BLK), BLK)] = (product * act[slot]).astype(BF16)
                else:
                    pre[slot] = value
            return carry

        lax.fori_loop(0, groups, multiply, 0)

    def out_copy(index, step, row, slot):
        return pltpu.make_async_remote_copy(
            src_ref=snd.at[index, row], dst_ref=rcv.at[index, slot],
            send_sem=out_send.at[index, step], recv_sem=out_recv.at[index, slot],
            device_id={"neuron": lax.rem(me + step, neurons)}, device_id_type=MESH,
        )

    def down_unit(index, carry):
        down_copy(index).wait()
        acc[...] = jnp.dot(hid[...], down_v[index], preferred_element_type=F32)

        def pack(part, inner):
            partial = acc[pl.ds(pl.multiple_of(part * 16, 16), 16), :]
            packed = partial.reshape(16, usubs, LANES).reshape(8, 2 * usubs, LANES)
            snd[index, pl.ds(part * 8, 8)] = packed.astype(BF16)
            return inner

        lax.fori_loop(0, neurons // 8, pack, 0)
        rcv[index, me] = snd[index, me]

        def send(step, inner):
            out_copy(index, step, lax.rem(me + step, neurons), me).start()
            return inner

        lax.fori_loop(1, neurons, send, 0, unroll=few)
        return carry

    lax.fori_loop(0, UNITS, down_unit, 0)

    def fin_copy(index):
        return pltpu.make_async_remote_copy(
            src_ref=rows_own.at[index], dst_ref=rows_other.at[index],
            send_sem=fin_send.at[index], recv_sem=fin_recv.at[index],
            device_id={"expert": other}, device_id_type=MESH,
        )

    upper = lax.broadcasted_iota(jnp.int32, (2 * usubs, LANES), 0) < usubs
    scale_rows = jnp.where(upper, scales[0], scales[1])

    def collect(index, carry):
        def arrive(step, inner):
            source = lax.rem(me + step, neurons)
            out_copy(index, step, source, source).wait_recv()
            return inner

        lax.fori_loop(1, neurons, arrive, 0, unroll=few)
        summed = jnp.sum(rcv[index].astype(F32), axis=0)
        rows_own[index] = summed * scale_rows
        fin_copy(index).start()
        return carry

    lax.fori_loop(0, UNITS, collect, 0)

    offset = (expert * per_dev).astype(F32)
    for index in range(UNITS):
        fin_copy(index).wait_recv()
        mine, others = rows_own[index], rows_other[index]
        tokens_out = []
        for token in range(per_dev):
            place = offset + float(token)
            value = jnp.zeros((usubs, LANES), F32)
            for source, pick_pair in ((mine, picks), (others, picks_other)):
                for row in range(2):
                    gain = (pick_pair[row] == place).astype(F32)
                    value = value + gain * source[row * usubs:(row + 1) * usubs, :]
            tokens_out.append(value[None])
        stacked = jnp.concatenate(tokens_out, axis=0).reshape(per_dev, unit)
        out_ref[:, index * unit:(index + 1) * unit] = stacked.astype(BF16)

    for index in range(UNITS):
        fin_copy(index).wait_send()

    def drain(index, carry):
        def leave(step, inner):
            out_copy(index, step, lax.rem(me + step, neurons), me).wait_send()
            return inner

        return lax.fori_loop(1, neurons, leave, carry, unroll=few)

    lax.fori_loop(0, UNITS, drain, 0)
    for part in range(PARTS + 1):
        def leave_token(step, carry, part=part):
            token_copy(part, step, me).wait_send()
            return carry

        lax.fori_loop(1, neurons, leave_token, 0, unroll=few)


def local(tokens, routes, route_weights, block_masks, block_list, gate_rows, up_rows, down_rows):
    routes, route_weights = routes.T, route_weights.T
    neurons = lax.axis_size("neuron")
    per_dev, width = tokens.shape
    held = gate_rows.shape[1]
    slots = held // BLK
    group_slots = max(size for size in (1, 3, 5) if slots % size == 0)
    rows = 2 * neurons
    subs = width // LANES
    unit = width // UNITS
    usubs = unit // LANES
    part_width = width // PARTS
    vmem = pl.BlockSpec(memory_space=pltpu.VMEM)
    hbm = pl.BlockSpec(memory_space=pl.ANY)
    dma = pltpu.SemaphoreType.DMA
    return pl.pallas_call(
        functools.partial(kernel, neurons, group_slots),
        out_shape=jax.ShapeDtypeStruct((per_dev, width), BF16),
        in_specs=[hbm] * 8,
        out_specs=vmem,
        scratch_shapes=[
            pltpu.VMEM((PARTS, slots, 2 * BLK, part_width), BF16),
            pltpu.VMEM((UNITS, held, unit), BF16),
            pltpu.VMEM((per_dev, width), BF16),
            pltpu.VMEM(block_list.shape, jnp.int32),
            pltpu.VMEM((2, per_dev, subs, LANES), BF16),
            pltpu.VMEM((2,) + routes.shape, jnp.int32),
            pltpu.VMEM((2,) + route_weights.shape, jnp.int32),
            pltpu.VMEM((2,) + block_masks.shape, jnp.int32),
            pltpu.VMEM((PARTS, neurons, 2 * subs // PARTS, LANES), BF16),
            pltpu.VMEM((neurons, 16, LANES), BF16),
            pltpu.VMEM((PARTS, rows, part_width), BF16),
            pltpu.VMEM((rows, LANES), F32),
            pltpu.VMEM((slots, rows, BLK), F32),
            pltpu.VMEM((slots, rows, 2 * BLK), F32),
            pltpu.VMEM((rows, held), BF16),
            pltpu.VMEM((rows, unit), F32),
            pltpu.VMEM((UNITS, neurons, 2 * usubs, LANES), BF16),
            pltpu.VMEM((UNITS, neurons, 2 * usubs, LANES), BF16),
            pltpu.VMEM((UNITS, 2 * usubs, LANES), F32),
            pltpu.VMEM((UNITS, 2 * usubs, LANES), F32),
            dma((PARTS, slots, 2)),
            dma((UNITS,)),
            dma((5,)),
            dma((4,)),
            dma((4,)),
            dma((PARTS + 1, neurons)),
            dma((PARTS + 1, neurons)),
            dma((UNITS, neurons)),
            dma((UNITS, neurons)),
            dma((UNITS,)),
            dma((UNITS,)),
        ],
        compiler_params=pltpu.CompilerParams(
            collective_id=0, has_side_effects=True, vmem_limit_bytes=58 * 1024 * 1024
        ),
    )(tokens, routes, route_weights, block_masks, block_list, gate_rows, up_rows, down_rows)


def solution(mesh):
    placed = (
        P(("groups", "neuron", "expert"), None),
        P(("groups", "neuron", "expert"), None),
        P(("groups", "neuron", "expert"), None),
        P(("groups", "neuron", "expert"), None, None),
        P(("groups", "expert"), None),
        P(("groups", "expert"), "neuron", None),
        P(("groups", "expert"), "neuron", None),
        P(("groups", "expert"), "neuron", None),
    )
    return jax.shard_map(
        local,
        mesh=mesh,
        in_specs=placed,
        out_specs=P(("groups", "neuron", "expert"), None),
        check_vma=False,
    )
```

```python
import functools

import jax
import jax.numpy as jnp
from jax import lax
from jax.experimental import pallas as pl
from jax.experimental.pallas import tpu as pltpu
from jax.sharding import PartitionSpec as P

BLK = 128
LANES = 128
UNITS = 2
PARTS = 2
TILE = 2 * BLK
CUT1 = 6
CUT2 = 8
F32 = jnp.float32
BF16 = jnp.bfloat16
MESH = pl.DeviceIdType.MESH


def total(value, axis):
    return jnp.sum(value, axis=axis, keepdims=True)


def picks_of(expert, routes, places):
    low, high = None, None
    for half in range(2):
        named = jnp.max((routes[half] == expert).astype(F32), axis=0, keepdims=True)
        least = jnp.min(jnp.where(named > 0.5, places[half], 1e6), axis=1, keepdims=True)
        most = jnp.max(jnp.where(named > 0.5, places[half], -1.0), axis=1, keepdims=True)
        low = least if low is None else jnp.minimum(low, least)
        high = most if high is None else jnp.maximum(high, most)
    return low, high


def kernel(
    neurons, group_slots,
    tok_in, routes_in, weights_in, masks_in, list_in, gate_hbm, up_hbm, down_hbm,
    out_ref,
    both_v, down_v, tok_v, list_v, pair_tok, pair_routes, pair_weights, pair_masks, slabs, slab_bits, lhs, bits_s,
    act, pre, hid, acc, snd, rcv, rows_own, rows_other,
    both_sem, down_sem, in_sem, pair_send, pair_recv, tok_send, tok_recv,
    out_send, out_recv, fin_send, fin_recv,
):
    me = lax.axis_index("neuron")
    expert = lax.axis_index("expert")
    other = 1 - expert
    per_dev, width = tok_in.shape
    subs = width // LANES
    part_width = width // PARTS
    part_subs = subs // PARTS
    unit = width // UNITS
    usubs = unit // LANES
    slots = both_v.shape[1]
    rows = 2 * neurons
    groups = slots // group_slots
    few = neurons <= 8

    barrier = pltpu.get_barrier_semaphore()

    def greet(step, carry):
        pl.semaphore_signal(
            barrier, inc=1, device_id={"neuron": lax.rem(me + step, neurons)}, device_id_type=MESH
        )
        return carry

    pl.semaphore_signal(barrier, inc=1, device_id={"expert": other}, device_id_type=MESH)
    lax.fori_loop(1, neurons, greet, 0, unroll=few)

    def small_copies():
        pairs = (
            (tok_in, tok_v), (routes_in, pair_routes.at[expert]), (weights_in, pair_weights.at[expert]),
            (masks_in, pair_masks.at[expert]), (list_in, list_v),
        )
        return [pltpu.make_async_copy(src, dst, in_sem.at[at]) for at, (src, dst) in enumerate(pairs)]

    for copy in small_copies():
        copy.start()

    def both_copies(part, slot):
        columns = pl.ds(pl.multiple_of(part * part_width, part_width), part_width)
        here = pl.ds(pl.multiple_of(slot * BLK, BLK), BLK)
        return [
            pltpu.make_async_copy(
                hbm.at[0, here, columns], both_v.at[part, slot, pl.ds(side * BLK, BLK), :],
                both_sem.at[part, slot, side],
            )
            for side, hbm in enumerate((gate_hbm, up_hbm))
        ]

    def down_copy(index):
        return pltpu.make_async_copy(
            down_hbm.at[0, :, pl.ds(index * unit, unit)], down_v.at[index], down_sem.at[index]
        )

    for part in range(PARTS):
        def begin(slot, carry, part=part):
            for copy in both_copies(part, slot):
                copy.start()
            return carry

        lax.fori_loop(0, slots, begin, 0)
    for index in range(UNITS):
        down_copy(index).start()

    for copy in small_copies():
        copy.wait()
    pair_tok[expert] = tok_v[...].astype(F32).reshape(per_dev, subs, LANES).astype(BF16)

    def turn(pair, carry):
        for inner in range(2):
            piece = 2 * pair + inner
            part = piece // slots
            slot = piece - part * slots
            for copy in both_copies(part, slot):
                copy.wait()
            for tile in range(part_width // TILE):
                here = slice(tile * TILE, (tile + 1) * TILE)
                both_v[part, slot, :, here] = both_v[part, slot, :, here].T
        return carry

    turned = [groups * group_slots, (groups // 3) * group_slots]
    if sum(turned) % 2:
        turned = [0, 0]
    pairs = sum(turned) // 2
    lax.fori_loop(0, pairs * CUT1 // 10, turn, 0)
    pl.semaphore_wait(barrier, neurons)

    def pair_copy(buffer, index):
        return pltpu.make_async_remote_copy(
            src_ref=buffer.at[expert], dst_ref=buffer.at[expert],
            send_sem=pair_send.at[index], recv_sem=pair_recv.at[index],
            device_id={"expert": other}, device_id_type=MESH,
        )

    pair_buffers = (pair_tok, pair_routes, pair_weights, pair_masks)
    for index, buffer in enumerate(pair_buffers):
        pair_copy(buffer, index).start()

    listed = list_v[...]
    slot_count = listed.shape[1]
    block_id = lax.broadcasted_iota(jnp.int32, (LANES, slot_count), 0)
    slot_id = lax.broadcasted_iota(jnp.int32, (LANES, slot_count), 1).astype(F32)
    first_slot = jnp.min(jnp.where(listed == block_id, slot_id, 1e6), axis=1, keepdims=True)
    own_slot = (lax.broadcasted_iota(jnp.int32, (LANES, LANES), 1) + me * slots).astype(F32)
    slot_lane = lax.broadcasted_iota(jnp.int32, (LANES, LANES), 1)
    holds = ((own_slot == first_slot) & (slot_lane < slots)).astype(F32).astype(BF16)

    lax.fori_loop(pairs * CUT1 // 10, pairs * CUT2 // 10, turn, 0)
    for index, buffer in enumerate(pair_buffers):
        pair_copy(buffer, index).wait()

    routes = [pair_routes[half] for half in range(2)]
    places = [
        lax.broadcasted_iota(jnp.int32, (1, per_dev), 1).astype(F32) + float(half * per_dev) for half in range(2)
    ]
    picks = picks_of(expert, routes, places)
    picks_other = picks_of(other, routes, places)

    def token_copy(part, step, source):
        buffer = slabs.at[part, source] if part < PARTS else slab_bits.at[source]
        return pltpu.make_async_remote_copy(
            src_ref=buffer, dst_ref=buffer,
            send_sem=tok_send.at[part, step], recv_sem=tok_recv.at[part, source],
            device_id={"neuron": lax.rem(me + step, neurons)}, device_id_type=MESH,
        )

    def token_start(part):
        def start(step, carry):
            token_copy(part, step, me).start()
            return carry

        lax.fori_loop(1, neurons, start, 0, unroll=few)

    def token_arrive(part):
        def arrive(step, carry):
            token_copy(part, step, lax.rem(me + step, neurons)).wait_recv()
            return carry

        lax.fori_loop(1, neurons, arrive, 0, unroll=few)

    gains = [[(pick == float(token)).astype(F32) for token in range(2 * per_dev)] for pick in picks]
    for part in range(PARTS):
        here = slice(part * part_subs, (part + 1) * part_subs)
        for row in range(2):
            chosen = jnp.zeros((part_subs, LANES), F32)
            for token in range(2 * per_dev):
                chosen = chosen + gains[row][token] * pair_tok[token // per_dev, token % per_dev, here, :].astype(F32)
            slabs[part, me, row * part_subs:(row + 1) * part_subs, :] = chosen.astype(BF16)
        token_start(part)

    lane = lax.broadcasted_iota(jnp.int32, (1, LANES), 1)
    word_of = sum((lane >= 30 * word).astype(jnp.int32) for word in (1, 2, 3))
    shift = jnp.minimum(lane - 30 * word_of, 30)
    scales, bit_rows = [], []
    for row, pick in enumerate(picks):
        scale, words = None, None
        for half in range(2):
            is_it = (routes[half] == expert) & (places[half] == pick)
            weight = total(total(jnp.where(is_it, pair_weights[half].astype(F32), 0.0), 0), 1)
            scale = weight if scale is None else scale + weight
            for token in range(per_dev):
                named = (routes[half][:, token:token + 1] == expert) & (gains[row][half * per_dev + token] > 0.5)
                word = jnp.where(named, pair_masks[half, token], 0)
                words = word if words is None else words + word
        words = total(words, 0)
        scales.append(scale / 65536.0)
        spread = jnp.where(
            word_of == 0, words[:, 0:1],
            jnp.where(word_of == 1, words[:, 1:2], jnp.where(word_of == 2, words[:, 2:3], words[:, 3:4])),
        )
        bit_rows.append(jnp.bitwise_and(jnp.right_shift(spread, shift), 1).astype(F32))
    line = lax.broadcasted_iota(jnp.int32, (16, LANES), 0)
    slab_bits[me] = jnp.where(line == 0, bit_rows[0], jnp.where(line == 1, bit_rows[1], 0.0)).astype(BF16)
    token_start(PARTS)

    def unpack(part):
        def piece(at, carry):
            arrived = slabs[part, pl.ds(at * 8, 8)].astype(F32)
            lhs[part, pl.ds(pl.multiple_of(at * 16, 16), 16), :] = (
                arrived.reshape(16, part_subs, LANES).reshape(16, part_width).astype(BF16)
            )
            return carry

        lax.fori_loop(0, neurons // 8, piece, 0)

    lax.fori_loop(pairs * CUT2 // 10, pairs, turn, 0)
    for part in range(PARTS):
        token_arrive(part)
        unpack(part)
        last = part == PARTS - 1
        if last:
            token_arrive(PARTS)
            for source in range(neurons):
                bits_s[2 * source:2 * source + 2, :] = slab_bits[source].astype(F32)[0:2, :]
            active = jnp.dot(bits_s[...].astype(BF16), holds, preferred_element_type=F32)
            for slot in range(slots):
                act[slot] = jnp.broadcast_to(active[:, slot:slot + 1], (rows, BLK))

        def multiply(group, carry, part, last, square):
            if not square:
                for inner in range(group_slots):
                    for copy in both_copies(part, group * group_slots + inner):
                        copy.wait()
            for inner in range(group_slots):
                slot = group * group_slots + inner
                value = pre[slot] if part > 0 else jnp.zeros((rows, 2 * BLK), F32)
                if not square:
                    contract = (((1,), (1,)), ((), ()))
                    value = value + lax.dot_general(
                        lhs[part], both_v[part, slot], contract, preferred_element_type=F32
                    )
                for tile in range(part_width // TILE if square else 0):
                    here = slice(tile * TILE, (tile + 1) * TILE)
                    value = value + jnp.dot(lhs[part, :, here], both_v[part, slot, :, here], preferred_element_type=F32)
                if last:
                    product = jnp.maximum(value[:, :BLK], 0.0) * jnp.maximum(value[:, BLK:], 0.0)
                    hid[:, pl.ds(pl.multiple_of(slot * BLK, BLK), BLK)] = (product * act[slot]).astype(BF16)
                else:
                    pre[slot] = value
            return carry

        ready = turned[part] // group_slots
        if ready:
            lax.fori_loop(0, ready, functools.partial(multiply, part=part, last=last, square=True), 0)
        if ready < groups:
            lax.fori_loop(ready, groups, functools.partial(multiply, part=part, last=last, square=False), 0)

    def out_copy(index, step, row, slot):
        return pltpu.make_async_remote_copy(
            src_ref=snd.at[index, row], dst_ref=rcv.at[index, slot],
            send_sem=out_send.at[index, step], recv_sem=out_recv.at[index, slot],
            device_id={"neuron": lax.rem(me + step, neurons)}, device_id_type=MESH,
        )

    def down_unit(index, carry):
        down_copy(index).wait()
        acc[...] = jnp.dot(hid[...], down_v[index], preferred_element_type=F32)

        def pack(part, inner):
            partial = acc[pl.ds(pl.multiple_of(part * 16, 16), 16), :]
            packed = partial.reshape(16, usubs, LANES).reshape(8, 2 * usubs, LANES)
            snd[index, pl.ds(part * 8, 8)] = packed.astype(BF16)
            return inner

        lax.fori_loop(0, neurons // 8, pack, 0)
        rcv[index, me] = snd[index, me]

        def send(step, inner):
            out_copy(index, step, lax.rem(me + step, neurons), me).start()
            return inner

        lax.fori_loop(1, neurons, send, 0, unroll=few)
        return carry

    lax.fori_loop(0, UNITS, down_unit, 0)

    def fin_copy(index):
        return pltpu.make_async_remote_copy(
            src_ref=rows_own.at[index], dst_ref=rows_other.at[index],
            send_sem=fin_send.at[index], recv_sem=fin_recv.at[index],
            device_id={"expert": other}, device_id_type=MESH,
        )

    upper = lax.broadcasted_iota(jnp.int32, (2 * usubs, LANES), 0) < usubs
    scale_rows = jnp.where(upper, scales[0], scales[1])

    def collect(index, carry):
        def arrive(step, inner):
            source = lax.rem(me + step, neurons)
            out_copy(index, step, source, source).wait_recv()
            return inner

        lax.fori_loop(1, neurons, arrive, 0, unroll=few)
        summed = jnp.sum(rcv[index].astype(F32), axis=0)
        rows_own[index] = summed * scale_rows
        fin_copy(index).start()
        return carry

    lax.fori_loop(0, UNITS, collect, 0)

    offset = (expert * per_dev).astype(F32)
    for index in range(UNITS):
        fin_copy(index).wait_recv()
        mine, others = rows_own[index], rows_other[index]
        tokens_out = []
        for token in range(per_dev):
            place = offset + float(token)
            value = jnp.zeros((usubs, LANES), F32)
            for source, pick_pair in ((mine, picks), (others, picks_other)):
                for row in range(2):
                    gain = (pick_pair[row] == place).astype(F32)
                    value = value + gain * source[row * usubs:(row + 1) * usubs, :]
            tokens_out.append(value[None])
        stacked = jnp.concatenate(tokens_out, axis=0).reshape(per_dev, unit)
        out_ref[:, index * unit:(index + 1) * unit] = stacked.astype(BF16)

    for index in range(UNITS):
        fin_copy(index).wait_send()

    def drain(index, carry):
        def leave(step, inner):
            out_copy(index, step, lax.rem(me + step, neurons), me).wait_send()
            return inner

        return lax.fori_loop(1, neurons, leave, carry, unroll=few)

    lax.fori_loop(0, UNITS, drain, 0)
    for part in range(PARTS + 1):
        def leave_token(step, carry, part=part):
            token_copy(part, step, me).wait_send()
            return carry

        lax.fori_loop(1, neurons, leave_token, 0, unroll=few)


def local(tokens, routes, route_weights, block_masks, block_list, gate_rows, up_rows, down_rows):
    routes, route_weights = routes.T, route_weights.T
    neurons = lax.axis_size("neuron")
    per_dev, width = tokens.shape
    held = gate_rows.shape[1]
    slots = held // BLK
    group_slots = max(size for size in (1, 3, 5) if slots % size == 0)
    rows = 2 * neurons
    subs = width // LANES
    unit = width // UNITS
    usubs = unit // LANES
    part_width = width // PARTS
    vmem = pl.BlockSpec(memory_space=pltpu.VMEM)
    hbm = pl.BlockSpec(memory_space=pl.ANY)
    dma = pltpu.SemaphoreType.DMA
    return pl.pallas_call(
        functools.partial(kernel, neurons, group_slots),
        out_shape=jax.ShapeDtypeStruct((per_dev, width), BF16),
        in_specs=[hbm] * 8,
        out_specs=vmem,
        scratch_shapes=[
            pltpu.VMEM((PARTS, slots, 2 * BLK, part_width), BF16),
            pltpu.VMEM((UNITS, held, unit), BF16),
            pltpu.VMEM((per_dev, width), BF16),
            pltpu.VMEM(block_list.shape, jnp.int32),
            pltpu.VMEM((2, per_dev, subs, LANES), BF16),
            pltpu.VMEM((2,) + routes.shape, jnp.int32),
            pltpu.VMEM((2,) + route_weights.shape, jnp.int32),
            pltpu.VMEM((2,) + block_masks.shape, jnp.int32),
            pltpu.VMEM((PARTS, neurons, 2 * subs // PARTS, LANES), BF16),
            pltpu.VMEM((neurons, 16, LANES), BF16),
            pltpu.VMEM((PARTS, rows, part_width), BF16),
            pltpu.VMEM((rows, LANES), F32),
            pltpu.VMEM((slots, rows, BLK), F32),
            pltpu.VMEM((slots, rows, 2 * BLK), F32),
            pltpu.VMEM((rows, held), BF16),
            pltpu.VMEM((rows, unit), F32),
            pltpu.VMEM((UNITS, neurons, 2 * usubs, LANES), BF16),
            pltpu.VMEM((UNITS, neurons, 2 * usubs, LANES), BF16),
            pltpu.VMEM((UNITS, 2 * usubs, LANES), F32),
            pltpu.VMEM((UNITS, 2 * usubs, LANES), F32),
            dma((PARTS, slots, 2)),
            dma((UNITS,)),
            dma((5,)),
            dma((4,)),
            dma((4,)),
            dma((PARTS + 1, neurons)),
            dma((PARTS + 1, neurons)),
            dma((UNITS, neurons)),
            dma((UNITS, neurons)),
            dma((UNITS,)),
            dma((UNITS,)),
        ],
        compiler_params=pltpu.CompilerParams(
            collective_id=0, has_side_effects=True, vmem_limit_bytes=58 * 1024 * 1024
        ),
    )(tokens, routes, route_weights, block_masks, block_list, gate_rows, up_rows, down_rows)


def solution(mesh):
    placed = (
        P(("groups", "neuron", "expert"), None),
        P(("groups", "neuron", "expert"), None),
        P(("groups", "neuron", "expert"), None),
        P(("groups", "neuron", "expert"), None, None),
        P(("groups", "expert"), None),
        P(("groups", "expert"), "neuron", None),
        P(("groups", "expert"), "neuron", None),
        P(("groups", "expert"), "neuron", None),
    )
    return jax.shard_map(
        local,
        mesh=mesh,
        in_specs=placed,
        out_specs=P(("groups", "neuron", "expert"), None),
        check_vma=False,
    )
```
